32 devices in a mesh: parts: 2 (over x), seq: 16 (over z, y, core).
Axes of the slice: x: 2, y: 2, z: 4, core: 2. Of those that a mesh axis runs over, the one named last changes fastest.
Arguments:
- frames: bfloat16 [8, 1024, 1024], P('parts', 'seq'), parts along dimension 0, may hold values from -10 to 10
- conv_weight: bfloat16 [128, 64, 1024], P('seq'), may hold values from -0.0625 to 0.0625
- conv_bias: float32 [1024], replicated, may hold values from -1 to 1
- w_qkv: bfloat16 [1024, 3, 16, 64], replicated, may hold values from -1 to 1
- w_out: bfloat16 [16, 64, 1024], replicated, may hold values from -1.5 to 1.5
Outputs:
- targets: bfloat16 [8, 1024, 1024], P('parts', 'seq'), parts along dimension 0
The draws below stay inside these ranges and needn't reach their ends.
There are 2 independent parts, one for each index of `parts`. The reference program is written for one: setup_inputs(seed, part) draws one part's arguments, and reference() takes and returns one part's arrays. A program takes and returns all parts, laid end to end along the dimension named above; an argument that names none is the same for every part. Nothing has to cross between parts.
All inputs are finite; a program needn't handle non-finite values.
Results may differ from the reference program's by a relative error of at most 0.012.
The reference program's roundings to bfloat16 on the way (of `mixed`, `qkv`, `probs` and `context`) count: a program that leaves them out, or rounds other values in their place, can miss the bound.
Values may be sent and summed in bfloat16 or wider, within the bound.
A program may use at most 192 MiB of HBM per device.

```python
import math
import jax
import jax.numpy as jnp
from jax import lax

D = 1024
HEADS = 16
GROUPS = 16
KERNEL = 128
HEAD = 64
REC = 4
LENGTH = 1024


def draw_frames(key, part):
    first = jax.random.fold_in(key, 0)
    return jnp.clip(jax.random.normal(first, (REC, LENGTH, D), jnp.float32), -6.0, 6.0).astype(jnp.bfloat16)


def draw_w_qkv(key, part):
    base = jax.random.normal(key, (D, 3, HEADS, HEAD), jnp.float32)
    base = jnp.clip(base, -6.0, 6.0) / math.sqrt(D)
    return base.astype(jnp.bfloat16)


def level_of(stream_key, shape, cuts, smallest, high):
    loudness = 1.0
    for dim, parts in cuts:
        steps = jax.random.uniform(jax.random.fold_in(jax.random.fold_in(stream_key, 6), dim), (parts,), jnp.float32, smallest / len(cuts), high / len(cuts))
        loudness = loudness * jnp.repeat(jnp.exp(steps), shape[dim] // parts).reshape((-1,) + (1,) * (len(shape) - 1 - dim))
    return loudness


def gaussian(own_key, shape, width, limit, cuts=(), kind=jnp.bfloat16):
    entries = jax.random.normal(own_key, shape, jnp.float32) * width
    if len(cuts) > 0:
        entries = level_of(own_key, shape, cuts, -0.22, 0.18) * entries
    return jnp.clip(entries, min=-limit, max=limit).astype(kind)


def setup_inputs(seed: int = 0, part: int = 0) -> dict:
    streams_of = jax.random.split(jax.random.key(seed), 6)
    part_keys = jax.random.split(jax.random.fold_in(streams_of[5], part), 6)
    return {
        "frames": draw_frames(jax.random.fold_in(jax.random.fold_in(streams_of[5], part), 71), part),
        "conv_weight": gaussian(streams_of[1], (KERNEL, D // GROUPS, D), (KERNEL * D // GROUPS) ** -0.5, 0.0625, ((0, 16),)),
        "conv_bias": jnp.clip(jax.random.uniform(streams_of[2], (D,), jnp.float32, -1.0, 1.0), -1.0, 1.0),
        "w_qkv": draw_w_qkv(jax.random.fold_in(streams_of[5], 71), part),
        "w_out": gaussian(streams_of[4], (HEADS, HEAD, D), 0.25, 1.5),
    }


def reference(frames, conv_weight, conv_bias, w_qkv, w_out):
    half = KERNEL // 2
    group_width = D // GROUPS
    padded = jnp.pad(frames, ((0, 0), (half, half), (0, 0))).astype(jnp.float32)
    grouped = padded.reshape(REC, LENGTH + KERNEL, GROUPS, group_width)
    kernel = conv_weight.astype(jnp.float32).reshape(KERNEL, group_width, GROUPS, group_width)

    def add_tap(tap, total):
        window = lax.dynamic_slice_in_dim(grouped, tap, LENGTH, 1)
        piece = lax.dynamic_index_in_dim(kernel, tap, 0, keepdims=False)
        return total + jnp.einsum('btgi,igo->btgo', window, piece)
    empty = jnp.zeros((REC, LENGTH, GROUPS, group_width), jnp.float32)
    conv = lax.fori_loop(0, KERNEL, add_tap, empty).reshape(REC, LENGTH, D) + conv_bias
    mixed = (frames.astype(jnp.float32) + jax.nn.gelu(conv)).astype(jnp.bfloat16)
    qkv = jnp.einsum('btd,dshe->bhtse', mixed.astype(jnp.float32), w_qkv.astype(jnp.float32)).astype(jnp.bfloat16)
    grid = qkv.reshape(REC * HEADS, LENGTH, 3, HEAD)
    scale = HEAD ** (-0.5)
    block = min(LENGTH, 512)

    def one(item):
        query = item[:, 0]
        keys = item[:, 1]
        values = item[:, 2]

        def rows(query_block):
            scores = jnp.einsum('qe,ke->qk', query_block.astype(jnp.float32), keys.astype(jnp.float32)) * scale
            top = lax.optimization_barrier(jnp.max(scores, axis=1, keepdims=True))
            weights = jnp.exp(scores - top)
            probs = (weights / lax.optimization_barrier(jnp.sum(weights, axis=1, keepdims=True))).astype(jnp.bfloat16)
            return jnp.dot(probs, values, preferred_element_type=jnp.float32).astype(jnp.bfloat16)
        return lax.map(rows, query.reshape(LENGTH // block, block, HEAD)).reshape(LENGTH, HEAD)
    context = lax.map(one, grid).reshape(REC, HEADS, LENGTH, HEAD)
    out = jnp.einsum('bhte,hed->btd', context.astype(jnp.float32), w_out.astype(jnp.float32))
    total = mixed.astype(jnp.float32) + out
    mean = lax.optimization_barrier(jnp.mean(total, axis=2, keepdims=True))
    centered = total - mean
    var = lax.optimization_barrier(jnp.mean(centered * centered, axis=2, keepdims=True))
    return (centered / jnp.sqrt(var + 1e-05)).astype(jnp.bfloat16)
```

```python
import functools
import math

import jax
import jax.numpy as jnp
from jax import lax
from jax.experimental import pallas as pl
from jax.experimental.pallas import tpu as pltpu
from jax.sharding import PartitionSpec as P

GROUPS = 16
KERNEL = 128
MESH = pl.DeviceIdType.MESH
F32 = jnp.float32
BF16 = jnp.bfloat16


def mm(a, b):
    return jnp.dot(a, b, preferred_element_type=F32)


def pair(a, b):
    w = a.shape[-1] // 2
    return (
        jnp.concatenate([a[:, :w], b[:, :w]], axis=1),
        jnp.concatenate([a[:, w:], b[:, w:]], axis=1),
    )


def fused_kernel(
    n, rec, groups, taps, head,
    x_ref, w_ref, bias_ref, wq_ref, wo_ref, out_ref,
    sx, rx, rf, xs, sw, ew, k2, mf, m4, gg, lhs, qkv, ct, cx, res,
    sx_send, sx_recv, sw_send, sw_recv, z_send, y_send, c_send, g_recv,
    r_send, r_recv, t_send, t_recv,
):
    me = lax.axis_index("seq")
    width = x_ref.shape[2]
    frames = x_ref.shape[1]
    gw = width // groups
    pack = 256 // gw
    vs = frames // pack
    rows = rec * vs
    per = n // rec
    wide = width // per
    tap_pairs = w_ref.shape[0] // 2
    own_rec = me // per
    own_h = me % per

    barrier = pltpu.get_barrier_semaphore()

    def greet(k, carry):
        pl.semaphore_signal(barrier, inc=1, device_id={"seq": (me + k) % n}, device_id_type=MESH)
        return carry

    lax.fori_loop(1, n, greet, 0)

    count = rec * frames
    ri = lax.broadcasted_iota(jnp.int32, (count, count), 0)
    ci = lax.broadcasted_iota(jnp.int32, (count, count), 1)
    a_i, rest = ri // rows, ri % rows
    r_i, v_i = rest // vs, rest % vs
    perm = jnp.where(ci == r_i * frames + v_i * pack + a_i, 1.0, 0.0).astype(BF16)
    x2 = x_ref[...].reshape(count, width)
    for gp in range(groups // 2):
        moved = mm(perm, x2[:, gp * 128:(gp + 1) * 128]).astype(BF16)
        for ah in range(pack // 2):
            lo, hi = pair(
                moved[2 * ah * rows:(2 * ah + 1) * rows],
                moved[(2 * ah + 1) * rows:(2 * ah + 2) * rows],
            )
            sx[2 * gp, :, ah * 128:(ah + 1) * 128] = lo
            sx[2 * gp + 1, :, ah * 128:(ah + 1) * 128] = hi

    pl.semaphore_wait(barrier, n - 1)

    def x_copy(peer, slot):
        return pltpu.make_async_remote_copy(
            src_ref=sx.at[peer], dst_ref=rx.at[slot],
            send_sem=sx_send.at[peer], recv_sem=sx_recv.at[slot],
            device_id={"seq": peer}, device_id_type=MESH,
        )

    def w_copy(peer, slot):
        return pltpu.make_async_remote_copy(
            src_ref=sw.at[peer], dst_ref=ew.at[pl.ds(1 + slot * tap_pairs, tap_pairs)],
            send_sem=sw_send.at[peer], recv_sem=sw_recv.at[slot],
            device_id={"seq": peer}, device_id_type=MESH,
        )

    def start_x(k, carry):
        x_copy((me + k) % n, me).start()
        return carry

    lax.fori_loop(1, n, start_x, 0)
    for p in range(tap_pairs):
        for gp in range(groups // 2):
            lo, hi = pair(
                w_ref[2 * p, :, gp * 128:(gp + 1) * 128],
                w_ref[2 * p + 1, :, gp * 128:(gp + 1) * 128],
            )
            sw[2 * gp, p] = lo
            sw[2 * gp + 1, p] = hi

    def start_w(k, carry):
        w_copy((me + k) % n, me).start()
        return carry

    lax.fori_loop(1, n, start_w, 0)

    rx[me] = sx[me]
    ew[pl.ds(1 + me * tap_pairs, tap_pairs)] = sw[me]
    ew[0] = jnp.zeros_like(ew[0])
    ew[taps // 2 + 1] = jnp.zeros_like(ew[0])
    zero = jnp.zeros((rows, 128), F32)
    for h in range(2):
        rf[h, 0:rows, :] = zero
        rf[h, (n + 1) * rows:(n + 2) * rows, :] = zero

    def wait_x(k, carry):
        x_copy((me + k) % n, (me + k) % n).wait_recv()
        return carry

    lax.fori_loop(1, n, wait_x, 0)

    def widen(s, carry):
        for h in range(2):
            rf[h, pl.ds((s + 1) * rows, rows), :] = rx[s, :, h * 128:(h + 1) * 128].astype(F32)
        return carry

    lax.fori_loop(0, n, widen, 0)

    def spread(k, carry):
        r, v = k // vs, k % vs
        for b in range(3):
            for h in range(2):
                val = rf[h, pl.ds(b * rows + k, n, stride=rows), :].astype(BF16)
                xs[pl.ds((vs * b + v) * (rec * n) + r * n, n), h * 128:(h + 1) * 128] = val
        return carry

    lax.fori_loop(0, rows, spread, 0)

    def wait_w(k, carry):
        w_copy((me + k) % n, (me + k) % n).wait_recv()
        return carry

    lax.fori_loop(1, n, wait_w, 0)

    blank = jnp.zeros((gw, 128), BF16)
    for j in range(3):
        k2[(taps + 1 + j) * gw:(taps + 2 + j) * gw, 0:128] = blank
    for j in (0, 1, taps + 3):
        k2[j * gw:(j + 1) * gw, 128:256] = blank
    low = lax.broadcasted_iota(jnp.int32, (gw, 128), 1) < gw

    def put(j, val):
        k2[pl.ds(j * gw, gw), 0:128] = val
        k2[pl.ds((j + 2) * gw, gw), 128:256] = val

    def even(p):
        return jnp.where(low, ew[p + 1].astype(F32), ew[p].astype(F32)).astype(BF16)

    def build(p, carry):
        put(2 * p, even(p))
        e = ew[p + 1]
        put(2 * p + 1, jnp.concatenate([e[:, gw:], e[:, :gw]], axis=1))
        return carry

    lax.fori_loop(0, taps // 2, build, 0)
    put(taps, even(taps // 2))

    total_rows = vs * rec * n
    chunk = total_rows // 2

    def conv(c, carry):
        base = c * chunk
        acc = jnp.zeros((chunk, 256), F32)
        for q in range(taps // pack + 1):
            acc += mm(xs[pl.ds(base + q * rec * n, chunk), :], k2[q * 256:(q + 1) * 256, :])
        centre = xs[pl.ds(base + vs * rec * n, chunk), :].astype(F32)
        mixed = (centre + jax.nn.gelu(acc + bias_ref[...])).astype(BF16).astype(F32)
        for h in range(2):
            mf[h, pl.ds(base, chunk), :] = mixed[:, h * 128:(h + 1) * 128]
        return carry

    lax.fori_loop(0, 2, conv, 0)

    def gather(k, carry):
        for h in range(2):
            val = mf[h, pl.ds(k, vs, stride=rec * n), :].astype(BF16)
            m4[k // n, pl.ds((k % n) * vs, vs), h * 128:(h + 1) * 128] = val
        return carry

    lax.fori_loop(0, rec * n, gather, 0)

    def z_copy(r, slot):
        return pltpu.make_async_remote_copy(
            src_ref=m4.at[r], dst_ref=gg.at[slot],
            send_sem=z_send.at[r], recv_sem=g_recv.at[slot],
            device_id={"seq": r * per + own_h}, device_id_type=MESH,
        )

    for d in range(1, rec):
        z_copy((own_rec + d) % rec, me).start()
    gg[me] = m4[own_rec]
    core, line = own_h % 2, own_h // 2
    lines = per // 2
    sibling = own_rec * per + line * 2 + 1 - core

    def y_copy(d, slot, sem):
        return pltpu.make_async_remote_copy(
            src_ref=gg.at[slot], dst_ref=gg.at[slot],
            send_sem=y_send.at[sem], recv_sem=g_recv.at[slot],
            device_id={"seq": own_rec * per + ((line + d) % lines) * 2 + core}, device_id_type=MESH,
        )

    def c_copy(slot):
        return pltpu.make_async_remote_copy(
            src_ref=gg.at[slot], dst_ref=gg.at[slot],
            send_sem=c_send.at[slot], recv_sem=g_recv.at[slot],
            device_id={"seq": sibling}, device_id_type=MESH,
        )

    for e in range(rec):
        z = (own_rec + e) % rec
        slot = z * per + own_h
        if e:
            z_copy(z, slot).wait_recv()
        for d in range(1, lines):
            y_copy(d, slot, (d - 1) * rec + e).start()
        c_copy(slot).start()
    for e in range(rec):
        z = (own_rec + e) % rec
        for d in range(1, lines):
            slot = z * per + ((line + d) % lines) * 2 + core
            y_copy(d, slot, (d - 1) * rec + e).wait_recv()
            c_copy(slot).start()
    for e in range(rec):
        z = (own_rec + e) % rec
        for d in range(lines):
            slot = z * per + ((line + d) % lines) * 2 + 1 - core
            c_copy(slot).wait_recv()

    span = n * vs
    for gp in range(groups // 2):
        for ah in range(pack // 2):
            lo, hi = pair(
                gg[2 * gp, :, ah * 128:(ah + 1) * 128], gg[2 * gp + 1, :, ah * 128:(ah + 1) * 128]
            )
            block, lane = (gp * 128) // wide, (gp * 128) % wide
            lhs[block, 2 * ah, :, lane:lane + 128] = lo
            lhs[block, 2 * ah + 1, :, lane:lane + 128] = hi

    def r_copy(u, slot):
        return pltpu.make_async_remote_copy(
            src_ref=lhs.at[own_h, :, pl.ds(pl.multiple_of(u * vs, vs), vs)],
            dst_ref=res.at[slot % per, slot // per],
            send_sem=r_send.at[u], recv_sem=r_recv.at[slot],
            device_id={"seq": u}, device_id_type=MESH,
        )

    def start_r(k, carry):
        r_copy((me + k) % n, me).start()
        return carry

    lax.fori_loop(1, n, start_r, 0)
    res[own_h, own_rec] = lhs[own_h, :, pl.ds(pl.multiple_of(me * vs, vs), vs), :]

    def project(a, carry):
        total = mm(lhs[0, a], wq_ref[0:wide, :])
        for b in range(1, per):
            total += mm(lhs[b, a], wq_ref[b * wide:(b + 1) * wide, :])
        qkv[pl.ds(a * span, span), :] = total.astype(BF16)
        return carry

    lax.fori_loop(0, pack, project, 0)

    def t_copy(a, u, slot):
        return pltpu.make_async_remote_copy(
            src_ref=ct.at[a, pl.ds(pl.multiple_of(u * vs, vs), vs)],
            dst_ref=cx.at[slot % per, slot // per, a],
            send_sem=t_send.at[a, u], recv_sem=t_recv.at[a, slot],
            device_id={"seq": u}, device_id_type=MESH,
        )

    lane = lax.broadcasted_iota(jnp.int32, (span, wide), 1) // head

    def attend(a, carry):
        query = qkv[pl.ds(a * span, span), 0:wide].astype(F32) * (head ** -0.5)
        done = jnp.zeros((span, wide), F32)
        for h in range(wide // head):
            mine = jnp.where(lane == h, query, 0.0).astype(BF16)
            scores = lax.dot_general(
                mine, qkv[:, wide:2 * wide], (((1,), (1,)), ((), ())), preferred_element_type=F32
            )
            weights = jnp.exp(scores - jnp.max(scores, axis=1, keepdims=True))
            inverse = 1.0 / jnp.sum(weights, axis=1, keepdims=True)
            probs = (weights * inverse).astype(BF16)
            done = jnp.where(lane == h, mm(probs, qkv[:, 2 * wide:3 * wide]), done)
        ct[a] = done.astype(BF16)

        def start_t(k, c):
            t_copy(a, (me + k) % n, me).start()
            return c

        lax.fori_loop(1, n, start_t, 0)
        cx[own_h, own_rec, a] = ct[a, pl.ds(pl.multiple_of(me * vs, vs), vs), :]
        return carry

    lax.fori_loop(0, pack, attend, 0)

    def wait_t(k, carry):
        s = (me + k) % n
        r_copy(s, s).wait_recv()
        for a in range(pack):
            t_copy(a, s, s).wait_recv()
        return carry

    lax.fori_loop(1, n, wait_t, 0)

    total = mm(cx[0].reshape(count, wide), wo_ref[0:wide, :])
    for b in range(1, per):
        total += mm(cx[b].reshape(count, wide), wo_ref[b * wide:(b + 1) * wide, :])
    total += jnp.concatenate([res[b].reshape(count, wide).astype(F32) for b in range(per)], axis=1)
    mean = jnp.mean(total, axis=1, keepdims=True)
    centred = total - mean
    var = jnp.mean(centred * centred, axis=1, keepdims=True)
    normed = (centred / jnp.sqrt(var + 1e-05)).astype(BF16)
    r_o, t_o = ri // frames, ri % frames
    back = jnp.where(ci == r_o * frames + (t_o % pack) * vs + t_o // pack, 1.0, 0.0).astype(BF16)
    out_ref[...] = mm(back, normed).astype(BF16).reshape(rec, frames, width)

    def drain(k, carry):
        s = (me + k) % n
        x_copy(s, me).wait_send()
        w_copy(s, me).wait_send()
        r_copy(s, me).wait_send()
        for a in range(pack):
            t_copy(a, s, me).wait_send()
        return carry

    lax.fori_loop(1, n, drain, 0)
    for e in range(rec):
        z = (own_rec + e) % rec
        if e:
            z_copy(z, me).wait_send()
        for d in range(1, lines):
            y_copy(d, z * per + own_h, (d - 1) * rec + e).wait_send()
        for d in range(lines):
            c_copy(z * per + ((line + d) % lines) * 2 + core).wait_send()


def fused(n, frames, conv_weight, conv_bias, w_qkv, w_out):
    rec, frame_count, width = frames.shape
    heads, head = w_qkv.shape[2:]
    groups, taps = GROUPS, KERNEL
    gw = width // groups
    pack = 256 // gw
    vs = frame_count // pack
    rows = rec * vs
    per = n // rec
    wide = width // per
    tap_pairs = conv_weight.shape[0] // 2
    me = lax.axis_index("seq")
    mine = heads // per
    w_mine = lax.dynamic_slice_in_dim(w_qkv, (me % per) * mine, mine, 2).reshape(width, 3 * mine * head)
    bias = lax.dynamic_slice_in_dim(conv_bias, me * gw, gw)
    bias = jnp.tile(bias, pack).reshape(1, 256)
    vm = lambda *s: pltpu.VMEM(s, BF16)
    dma = lambda *s: pltpu.SemaphoreType.DMA(s)
    lines = per // 2
    return pl.pallas_call(
        functools.partial(fused_kernel, n, rec, groups, taps, head),
        out_shape=jax.ShapeDtypeStruct(frames.shape, BF16),
        in_specs=[pl.BlockSpec(memory_space=pltpu.VMEM)] * 5,
        out_specs=pl.BlockSpec(memory_space=pltpu.VMEM),
        scratch_shapes=[
            vm(n, rows, 256), vm(n, rows, 256), pltpu.VMEM((2, (n + 2) * rows, 128), F32),
            vm(3 * vs * rec * n, 256), vm(n, tap_pairs, gw, 128), vm(taps // 2 + 2, gw, 128),
            vm((taps + 4) * gw, 256), pltpu.VMEM((2, vs * rec * n, 128), F32),
            vm(rec, n * vs, 256), vm(n, n * vs, 256), vm(per, pack, n * vs, wide),
            vm(pack * n * vs, 3 * wide), vm(pack, n * vs, wide),
            vm(per, rec, pack, vs, wide), vm(per, rec, pack, vs, wide),
            dma(n), dma(n), dma(n), dma(n), dma(rec), dma(max(1, (lines - 1) * rec)), dma(n), dma(n),
            dma(n), dma(n), dma(pack, n), dma(pack, n),
        ],
        compiler_params=pltpu.CompilerParams(
            collective_id=0, has_side_effects=True, vmem_limit_bytes=56 * 2 ** 20
        ),
    )(frames, conv_weight, bias, w_mine, w_out.reshape(width, width))


def conv_part(source, kernel, groups):
    return lax.conv_general_dilated(
        source,
        kernel,
        (1,),
        "VALID",
        dimension_numbers=("NWC", "WIO", "NWC"),
        feature_group_count=groups,
        preferred_element_type=jnp.float32,
    )


def fits(n, frames, conv_weight, w_qkv):
    rec, frame_count, width = frames.shape
    heads, head = w_qkv.shape[2:]
    return (
        n == GROUPS
        and width == heads * head
        and width == GROUPS * 64
        and frame_count == KERNEL // 2
        and n % (2 * rec) == 0
        and heads % (n // rec) == 0
        and width * rec == 256 * n
    )


def body(frames, conv_weight, conv_bias, w_qkv, w_out):
    rec, frame_count, width = frames.shape
    devices = lax.axis_size("seq")
    if fits(devices, frames, conv_weight, w_qkv):
        return fused(devices, frames, conv_weight, conv_bias, w_qkv, w_out)
    group_width = width // GROUPS
    half = KERNEL // 2
    blocks = devices // GROUPS
    per_dev = rec // blocks
    tap_count = conv_weight.shape[0]
    spread = conv_weight.reshape(tap_count, group_width, 1, GROUPS, group_width)
    spread = jnp.broadcast_to(spread, (tap_count, group_width, blocks, GROUPS, group_width))
    spread = spread.reshape(tap_count, group_width, devices, group_width)
    kernel = lax.all_to_all(spread, "seq", split_axis=2, concat_axis=0, tiled=True).reshape(
        KERNEL, group_width, group_width
    )
    arranged = frames.reshape(blocks, per_dev, frame_count, GROUPS, group_width)
    arranged = jnp.transpose(arranged, (0, 3, 1, 2, 4)).reshape(
        devices, per_dev, frame_count, group_width
    )
    length = frame_count * devices
    inputs = lax.all_to_all(arranged, "seq", split_axis=0, concat_axis=2, tiled=True).reshape(
        per_dev, length, group_width
    )
    padded = jnp.pad(inputs, ((0, 0), (half, half - 1), (0, 0)))
    conv = conv_part(padded, kernel, 1)
    group_index = lax.axis_index("seq") % GROUPS
    bias = lax.dynamic_slice_in_dim(conv_bias, group_index * group_width, group_width)
    local = (inputs.astype(jnp.float32) + jax.nn.gelu(conv + bias)).astype(jnp.bfloat16)
    sending = local.reshape(1, per_dev, devices, frame_count, group_width)
    returned = lax.all_to_all(sending, "seq", split_axis=2, concat_axis=0, tiled=True)
    returned = returned.reshape(blocks, GROUPS, per_dev, frame_count, group_width)
    mixed = jnp.transpose(returned, (0, 2, 3, 1, 4)).reshape(rec, frame_count, width)
    heads = w_qkv.shape[2]
    head = w_qkv.shape[3]
    items = rec * heads // devices
    projected = jnp.einsum(
        "btd,dshe->bhtse", mixed, w_qkv, preferred_element_type=jnp.float32
    ).astype(jnp.bfloat16)
    packed = projected.reshape(devices, items, frame_count, 3 * head)
    scale = head ** (-0.5)
    portion = lax.all_to_all(packed, "seq", split_axis=0, concat_axis=2, tiled=True)
    count = portion.shape[1]
    length = portion.shape[2]
    grid = portion.reshape(count, length, 3, head)
    block = math.gcd(length, 512)

    def one(item):
        query = item[:, 0]
        keys = item[:, 1]
        values = item[:, 2]

        def rows(query_block):
            scores = (
                jnp.einsum("qe,ke->qk", query_block, keys, preferred_element_type=jnp.float32)
                * scale
            )
            top = jnp.max(scores, axis=1, keepdims=True)
            weights = jnp.exp(scores - top)
            probs = (weights / jnp.sum(weights, axis=1, keepdims=True)).astype(jnp.bfloat16)
            return jnp.dot(probs, values, preferred_element_type=jnp.float32).astype(jnp.bfloat16)

        return lax.map(rows, query.reshape(length // block, block, head)).reshape(length, head)

    attended = lax.map(one, grid)
    context = lax.all_to_all(attended[None], "seq", split_axis=2, concat_axis=0, tiled=True)
    context = context.reshape(rec, heads, frame_count, head)
    out = jnp.einsum("bhte,hed->btd", context, w_out, preferred_element_type=jnp.float32)
    total = mixed.astype(jnp.float32) + out
    mean = jnp.mean(total, axis=2, keepdims=True)
    centered = total - mean
    var = jnp.mean(centered * centered, axis=2, keepdims=True)
    return (centered / jnp.sqrt(var + 1e-05)).astype(jnp.bfloat16)


def solution(mesh):
    return jax.shard_map(
        body,
        mesh=mesh,
        in_specs=(P("parts", "seq", None), P("seq", None, None), P(), P(), P()),
        out_specs=P("parts", "seq", None),
        check_vma=False,
    )
```

```python
import functools
import math

import jax
import jax.numpy as jnp
from jax import lax
from jax.experimental import pallas as pl
from jax.experimental.pallas import tpu as pltpu
from jax.sharding import PartitionSpec as P

GROUPS = 16
KERNEL = 128
MESH = pl.DeviceIdType.MESH
F32 = jnp.float32
BF16 = jnp.bfloat16


def mm(a, b):
    return jnp.dot(a, b, preferred_element_type=F32)


def pair(a, b):
    w = a.shape[-1] // 2
    return (
        jnp.concatenate([a[:, :w], b[:, :w]], axis=1),
        jnp.concatenate([a[:, w:], b[:, w:]], axis=1),
    )


def fused_kernel(
    n, parts, rec, groups, taps, head,
    x_ref, w_ref, bias_ref, wq_hbm, wo_hbm, out_ref,
    sx, rx, rf, xs, sw, ew, k2, mf, m4, gg, lhs, qacc, qkv, ct, cx, res, wq_ref, wo_ref,
    sx_send, sx_recv, sw_send, sw_recv, f_send, f_recv, z_send, y_send, c_send, g_recv,
    r_send, r_recv, t_send, t_recv, l_sem,
):
    me = lax.axis_index("seq")
    width = x_ref.shape[2]
    frames = x_ref.shape[1]
    gw = width // groups
    pack = 256 // gw
    vs = frames // pack
    rows = rec * vs
    per = n // rec
    wide = width // per
    tap_pairs = w_ref.shape[0] // 2
    share = tap_pairs // parts
    part = lax.axis_index("parts") if parts > 1 else 0
    own_rec = me // per
    own_h = me % per

    barrier = pltpu.get_barrier_semaphore()

    def greet(k, carry):
        pl.semaphore_signal(barrier, inc=1, device_id={"seq": (me + k) % n}, device_id_type=MESH)
        return carry

    lax.fori_loop(1, n, greet, 0)
    for d in range(1, parts):
        pl.semaphore_signal(
            barrier, inc=1, device_id={"parts": (part + d) % parts, "seq": me}, device_id_type=MESH
        )
    wq_load = pltpu.make_async_copy(wq_hbm, wq_ref, l_sem.at[0])
    wo_load = pltpu.make_async_copy(wo_hbm, wo_ref, l_sem.at[1])

    def x_copy(peer, slot):
        return pltpu.make_async_remote_copy(
            src_ref=sx.at[peer], dst_ref=rx.at[slot],
            send_sem=sx_send.at[peer], recv_sem=sx_recv.at[slot],
            device_id={"seq": peer}, device_id_type=MESH,
        )

    def w_copy(peer, slot):
        return pltpu.make_async_remote_copy(
            src_ref=sw.at[peer], dst_ref=ew.at[pl.ds(1 + slot * tap_pairs + part * share, share)],
            send_sem=sw_send.at[peer], recv_sem=sw_recv.at[slot],
            device_id={"seq": peer}, device_id_type=MESH,
        )

    for p in range(share):
        for gp in range(groups // 2):
            tap = 2 * (part * share + p)
            lo, hi = pair(
                w_ref[tap, :, gp * 128:(gp + 1) * 128], w_ref[tap + 1, :, gp * 128:(gp + 1) * 128]
            )
            sw[2 * gp, p] = lo
            sw[2 * gp + 1, p] = hi

    pl.semaphore_wait(barrier, n - 1 + parts - 1)

    def start_w(k, carry):
        w_copy((me + k) % n, me).start()
        return carry

    lax.fori_loop(1, n, start_w, 0)

    ew[pl.ds(1 + me * tap_pairs + part * share, share)] = sw[me]

    def f_copy(d, slot):
        return pltpu.make_async_remote_copy(
            src_ref=ew.at[pl.ds(1 + slot * tap_pairs + part * share, share)],
            dst_ref=ew.at[pl.ds(1 + slot * tap_pairs + part * share, share)],
            send_sem=f_send.at[d - 1, slot], recv_sem=f_recv.at[d - 1, slot],
            device_id={"parts": (part + d) % parts, "seq": me}, device_id_type=MESH,
        )

    def f_wait(d, slot):
        source = (part + parts - d) % parts
        return pltpu.make_async_remote_copy(
            src_ref=ew.at[pl.ds(1 + slot * tap_pairs + source * share, share)],
            dst_ref=ew.at[pl.ds(1 + slot * tap_pairs + source * share, share)],
            send_sem=f_send.at[d - 1, slot], recv_sem=f_recv.at[d - 1, slot],
            device_id={"parts": (part + d) % parts, "seq": me}, device_id_type=MESH,
        )

    for d in range(1, parts):
        f_copy(d, me).start()

    count = rec * frames
    ri = lax.broadcasted_iota(jnp.int32, (count, count), 0)
    ci = lax.broadcasted_iota(jnp.int32, (count, count), 1)
    a_i, rest = ri // rows, ri % rows
    r_i, v_i = rest // vs, rest % vs
    perm = jnp.where(ci == r_i * frames + v_i * pack + a_i, 1.0, 0.0).astype(BF16)
    x2 = x_ref[...].reshape(count, width)
    for gp in range(groups // 2):
        moved = mm(perm, x2[:, gp * 128:(gp + 1) * 128]).astype(BF16)
        for ah in range(pack // 2):
            lo, hi = pair(
                moved[2 * ah * rows:(2 * ah + 1) * rows],
                moved[(2 * ah + 1) * rows:(2 * ah + 2) * rows],
            )
            sx[2 * gp, :, ah * 128:(ah + 1) * 128] = lo
            sx[2 * gp + 1, :, ah * 128:(ah + 1) * 128] = hi

    def start_x(k, carry):
        x_copy((me + k) % n, me).start()
        return carry

    lax.fori_loop(1, n, start_x, 0)
    wq_load.start()
    wo_load.start()
    rx[me] = sx[me]
    ew[0] = jnp.zeros_like(ew[0])
    ew[taps // 2 + 1] = jnp.zeros_like(ew[0])
    zero = jnp.zeros((rows, 128), F32)
    for h in range(2):
        rf[h, 0:rows, :] = zero
        rf[h, (n + 1) * rows:(n + 2) * rows, :] = zero

    def wait_w(k, carry):
        s = (me + n - k) % n
        w_copy(s, s).wait_recv()
        for d in range(1, parts):
            f_copy(d, s).start()
        return carry

    lax.fori_loop(1, n, wait_w, 0)

    def wait_f(k, carry):
        for d in range(1, parts):
            f_wait(d, (me + n - k) % n).wait_recv()
        return carry

    lax.fori_loop(0, n, wait_f, 0)

    blank = jnp.zeros((gw, 128), BF16)
    for j in range(3):
        k2[(taps + 1 + j) * gw:(taps + 2 + j) * gw, 0:128] = blank
    for j in (0, 1, taps + 3):
        k2[j * gw:(j + 1) * gw, 128:256] = blank
    low = lax.broadcasted_iota(jnp.int32, (gw, 128), 1) < gw

    def put(j, val):
        k2[pl.ds(j * gw, gw), 0:128] = val
        k2[pl.ds((j + 2) * gw, gw), 128:256] = val

    def even(p):
        return jnp.where(low, ew[p + 1].astype(F32), ew[p].astype(F32)).astype(BF16)

    def build(p, carry):
        put(2 * p, even(p))
        e = ew[p + 1]
        put(2 * p + 1, jnp.concatenate([e[:, gw:], e[:, :gw]], axis=1))
        return carry

    lax.fori_loop(0, taps // 2, build, 0)
    put(taps, even(taps // 2))

    def widen(k, carry):
        s = (me + n - k) % n

        @pl.when(k > 0)
        def _():
            x_copy(s, s).wait_recv()

        for h in range(2):
            rf[h, pl.ds((s + 1) * rows, rows), :] = rx[s, :, h * 128:(h + 1) * 128].astype(F32)
        return carry

    lax.fori_loop(0, n, widen, 0)

    def spread(k, carry):
        r, v = k // vs, k % vs
        for b in range(3):
            for h in range(2):
                val = rf[h, pl.ds(b * rows + k, n, stride=rows), :].astype(BF16)
                xs[vs * b + v, r, :, h * 128:(h + 1) * 128] = val
        return carry

    lax.fori_loop(0, rows, spread, 0)

    pairs = rec // 2
    chunk = vs * 2 * n
    w2 = bias_ref[:, pl.ds(pl.multiple_of((me // 2) * 128, 128), 128)]
    lo, hi = pair(w2, w2)
    bias = jnp.where(me % 2 == 0, lo, hi)
    bias = jnp.concatenate([bias, bias], axis=1)

    def z_copy(r, slot):
        return pltpu.make_async_remote_copy(
            src_ref=m4.at[r], dst_ref=gg.at[slot],
            send_sem=z_send.at[r], recv_sem=g_recv.at[slot],
            device_id={"seq": r * per + own_h}, device_id_type=MESH,
        )

    for i in range(pairs):
        cp = (own_rec // 2 + 1 + i) % pairs
        acc = jnp.zeros((chunk, 256), F32)
        for q in range(taps // pack + 1):
            acc += mm(
                xs[q:q + vs, pl.ds(2 * cp, 2)].reshape(chunk, 256), k2[q * 256:(q + 1) * 256, :]
            )
        centre = xs[vs:2 * vs, pl.ds(2 * cp, 2)].reshape(chunk, 256).astype(F32)
        mixed = (centre + jax.nn.gelu(acc + bias)).astype(BF16).astype(F32)
        for h in range(2):
            mf[h] = mixed[:, h * 128:(h + 1) * 128]

        def gather(k, carry):
            for h in range(2):
                val = mf[h, pl.ds(k, vs, stride=2 * n), :].astype(BF16)
                m4[2 * cp + k // n, pl.ds((k % n) * vs, vs), h * 128:(h + 1) * 128] = val
            return carry

        lax.fori_loop(0, 2 * n, gather, 0)
        for j in range(2):
            if i < pairs - 1 or j:
                z_copy(2 * cp + (own_rec + j) % 2, me).start()
    gg[me] = m4[own_rec]
    core, line = own_h % 2, own_h // 2
    lines = per // 2
    sibling = own_rec * per + line * 2 + 1 - core

    def y_copy(d, slot, sem):
        return pltpu.make_async_remote_copy(
            src_ref=gg.at[slot], dst_ref=gg.at[slot],
            send_sem=y_send.at[sem], recv_sem=g_recv.at[slot],
            device_id={"seq": own_rec * per + ((line + d) % lines) * 2 + core}, device_id_type=MESH,
        )

    def c_copy(slot):
        return pltpu.make_async_remote_copy(
            src_ref=gg.at[slot], dst_ref=gg.at[slot],
            send_sem=c_send.at[slot], recv_sem=g_recv.at[slot],
            device_id={"seq": sibling}, device_id_type=MESH,
        )

    wq_load.wait()
    wo_load.wait()
    span = n * vs

    def step_a(e, z):
        slot = z * per + own_h
        if e:
            z_copy(z, slot).wait_recv()
        for d in range(1, lines):
            y_copy(d, slot, (d - 1) * rec + e).start()
        c_copy(slot).start()

    def step_b(e, z):
        for d in range(1, lines):
            slot = z * per + ((line + d) % lines) * 2 + core
            y_copy(d, slot, (d - 1) * rec + e).wait_recv()
            c_copy(slot).start()

    def step_c(e, z):
        for d in range(lines):
            c_copy(z * per + ((line + d) % lines) * 2 + 1 - core).wait_recv()
        for gl in range(per // 2):
            for ah in range(pack // 2):
                g = z * per + 2 * gl
                lo, hi = pair(
                    gg[g, :, ah * 128:(ah + 1) * 128], gg[g + 1, :, ah * 128:(ah + 1) * 128]
                )
                lhs[z, 2 * ah, :, gl * 128:(gl + 1) * 128] = lo
                lhs[z, 2 * ah + 1, :, gl * 128:(gl + 1) * 128] = hi

        def project(a, carry):
            at = pl.ds(a * span, span)
            total = mm(lhs[z, a], wq_ref[pl.ds(pl.multiple_of(z * wide, wide), wide), :])
            if e:
                total += qacc[at, :]
            if e == rec - 1:
                qkv[at, :] = total.astype(BF16)
            else:
                qacc[at, :] = total
            return carry

        lax.fori_loop(0, pack, project, 0)

    mate = (own_rec // 2) * 2 + 1 - own_rec % 2
    others = [
        2 * ((own_rec // 2 + 1 + i) % pairs) + (own_rec + j) % 2
        for i in range(pairs - 1) for j in range(2)
    ]
    zs = list(enumerate([own_rec] + others + [mate]))
    for e, z in zs[:-1]:
        step_a(e, z)
    for e, z in zs[:-1]:
        step_b(e, z)
    step_a(*zs[-1])
    for e, z in zs[:-2]:
        step_c(e, z)
    step_b(*zs[-1])
    for e, z in zs[-2:]:
        step_c(e, z)

    def r_copy(u, slot):
        return pltpu.make_async_remote_copy(
            src_ref=lhs.at[own_h, :, pl.ds(pl.multiple_of(u * vs, vs), vs)],
            dst_ref=res.at[slot % per, slot // per],
            send_sem=r_send.at[u], recv_sem=r_recv.at[slot],
            device_id={"seq": u}, device_id_type=MESH,
        )

    def start_r(k, carry):
        r_copy((me + k) % n, me).start()
        return carry

    lax.fori_loop(1, n, start_r, 0)
    res[own_h, own_rec] = lhs[own_h, :, pl.ds(pl.multiple_of(me * vs, vs), vs), :]

    def t_copy(a, u, slot):
        return pltpu.make_async_remote_copy(
            src_ref=ct.at[a, pl.ds(pl.multiple_of(u * vs, vs), vs)],
            dst_ref=cx.at[slot % per, slot // per, a],
            send_sem=t_send.at[a, u], recv_sem=t_recv.at[a, slot],
            device_id={"seq": u}, device_id_type=MESH,
        )

    lane = lax.broadcasted_iota(jnp.int32, (span, wide), 1) // head

    def attend(a, carry):
        query = qkv[pl.ds(a * span, span), 0:wide].astype(F32) * (head ** -0.5)
        done = jnp.zeros((span, wide), F32)
        for h in range(wide // head):
            mine = jnp.where(lane == h, query, 0.0).astype(BF16)
            scores = lax.dot_general(
                mine, qkv[:, wide:2 * wide], (((1,), (1,)), ((), ())), preferred_element_type=F32
            )
            weights = jnp.exp(scores - jnp.max(scores, axis=1, keepdims=True))
            inverse = 1.0 / jnp.sum(weights, axis=1, keepdims=True)
            probs = (weights * inverse).astype(BF16)
            done = jnp.where(lane == h, mm(probs, qkv[:, 2 * wide:3 * wide]), done)
        ct[a] = done.astype(BF16)

        def start_t(k, c):
            t_copy(a, (me + k) % n, me).start()
            return c

        lax.fori_loop(1, n, start_t, 0)
        cx[own_h, own_rec, a] = ct[a, pl.ds(pl.multiple_of(me * vs, vs), vs), :]
        return carry

    lax.fori_loop(0, pack, attend, 0)

    def wait_t(k, carry):
        s = (me + k) % n
        r_copy(s, s).wait_recv()
        for a in range(pack):
            t_copy(a, s, s).wait_recv()
        return carry

    lax.fori_loop(1, n, wait_t, 0)

    total = mm(cx[0].reshape(count, wide), wo_ref[0:wide, :])
    for b in range(1, per):
        total += mm(cx[b].reshape(count, wide), wo_ref[b * wide:(b + 1) * wide, :])
    total += jnp.concatenate([res[b].reshape(count, wide).astype(F32) for b in range(per)], axis=1)
    mean = jnp.mean(total, axis=1, keepdims=True)
    centred = total - mean
    var = jnp.mean(centred * centred, axis=1, keepdims=True)
    normed = (centred / jnp.sqrt(var + 1e-05)).astype(BF16)
    r_o, t_o = ri // frames, ri % frames
    back = jnp.where(ci == r_o * frames + (t_o % pack) * vs + t_o // pack, 1.0, 0.0).astype(BF16)
    out_ref[...] = mm(back, normed).astype(BF16).reshape(rec, frames, width)

    def drain(k, carry):
        s = (me + k) % n
        x_copy(s, me).wait_send()
        w_copy(s, me).wait_send()
        r_copy(s, me).wait_send()
        for a in range(pack):
            t_copy(a, s, me).wait_send()
        return carry

    lax.fori_loop(1, n, drain, 0)
    for d in range(1, parts):
        for s in range(n):
            f_copy(d, s).wait_send()
    for e, z in zs:
        if e:
            z_copy(z, me).wait_send()
        for d in range(1, lines):
            y_copy(d, z * per + own_h, (d - 1) * rec + e).wait_send()
        for d in range(lines):
            c_copy(z * per + ((line + d) % lines) * 2 + core).wait_send()


def fused(n, frames, conv_weight, conv_bias, w_qkv, w_out):
    rec, frame_count, width = frames.shape
    heads, head = w_qkv.shape[2:]
    groups, taps = GROUPS, KERNEL
    gw = width // groups
    pack = 256 // gw
    vs = frame_count // pack
    rows = rec * vs
    per = n // rec
    wide = width // per
    tap_pairs = conv_weight.shape[0] // 2
    me = lax.axis_index("seq")
    mine = heads // per
    w_mine = lax.dynamic_slice_in_dim(w_qkv, (me % per) * mine, mine, 2).reshape(width, 3 * mine * head)
    bias = conv_bias.reshape(1, width)
    parts = lax.axis_size("parts")
    if tap_pairs % parts:
        parts = 1
    vm = lambda *s: pltpu.VMEM(s, BF16)
    dma = lambda *s: pltpu.SemaphoreType.DMA(s)
    lines = per // 2
    return pl.pallas_call(
        functools.partial(fused_kernel, n, parts, rec, groups, taps, head),
        out_shape=jax.ShapeDtypeStruct(frames.shape, BF16),
        in_specs=[pl.BlockSpec(memory_space=pltpu.VMEM)] * 3 + [pl.BlockSpec(memory_space=pl.ANY)] * 2,
        out_specs=pl.BlockSpec(memory_space=pltpu.VMEM),
        scratch_shapes=[
            vm(n, rows, 256), vm(n, rows, 256), pltpu.VMEM((2, (n + 2) * rows, 128), F32),
            vm(3 * vs, rec, n, 256), vm(n, tap_pairs // parts, gw, 128), vm(taps // 2 + 2, gw, 128),
            vm((taps + 4) * gw, 256), pltpu.VMEM((2, vs * 2 * n, 128), F32),
            vm(rec, n * vs, 256), vm(n, n * vs, 256), vm(per, pack, n * vs, wide),
            pltpu.VMEM((pack * n * vs, 3 * wide), F32), vm(pack * n * vs, 3 * wide), vm(pack, n * vs, wide),
            vm(per, rec, pack, vs, wide), vm(per, rec, pack, vs, wide),
            vm(width, 3 * wide), vm(width, width),
            dma(n), dma(n), dma(n), dma(n),
            dma(max(1, parts - 1), n), dma(max(1, parts - 1), n), dma(rec), dma(max(1, (lines - 1) * rec)), dma(n), dma(n),
            dma(n), dma(n), dma(pack, n), dma(pack, n), dma(2),
        ],
        compiler_params=pltpu.CompilerParams(
            collective_id=0, has_side_effects=True, vmem_limit_bytes=56 * 2 ** 20
        ),
    )(frames, conv_weight, bias, w_mine, w_out.reshape(width, width))


def conv_part(source, kernel, groups):
    return lax.conv_general_dilated(
        source,
        kernel,
        (1,),
        "VALID",
        dimension_numbers=("NWC", "WIO", "NWC"),
        feature_group_count=groups,
        preferred_element_type=jnp.float32,
    )


def fits(n, frames, conv_weight, w_qkv):
    rec, frame_count, width = frames.shape
    heads, head = w_qkv.shape[2:]
    return (
        n == GROUPS
        and width == heads * head
        and width == GROUPS * 64
        and frame_count == KERNEL // 2
        and n % (2 * rec) == 0
        and rec % 2 == 0
        and n * 64 == 256 * rec
        and conv_weight.shape[0] % 2 == 0
        and heads % (n // rec) == 0
        and width * rec == 256 * n
    )


def body(frames, conv_weight, conv_bias, w_qkv, w_out):
    rec, frame_count, width = frames.shape
    devices = lax.axis_size("seq")
    if fits(devices, frames, conv_weight, w_qkv):
        return fused(devices, frames, conv_weight, conv_bias, w_qkv, w_out)
    group_width = width // GROUPS
    half = KERNEL // 2
    blocks = devices // GROUPS
    per_dev = rec // blocks
    tap_count = conv_weight.shape[0]
    spread = conv_weight.reshape(tap_count, group_width, 1, GROUPS, group_width)
    spread = jnp.broadcast_to(spread, (tap_count, group_width, blocks, GROUPS, group_width))
    spread = spread.reshape(tap_count, group_width, devices, group_width)
    kernel = lax.all_to_all(spread, "seq", split_axis=2, concat_axis=0, tiled=True).reshape(
        KERNEL, group_width, group_width
    )
    arranged = frames.reshape(blocks, per_dev, frame_count, GROUPS, group_width)
    arranged = jnp.transpose(arranged, (0, 3, 1, 2, 4)).reshape(
        devices, per_dev, frame_count, group_width
    )
    length = frame_count * devices
    inputs = lax.all_to_all(arranged, "seq", split_axis=0, concat_axis=2, tiled=True).reshape(
        per_dev, length, group_width
    )
    padded = jnp.pad(inputs, ((0, 0), (half, half - 1), (0, 0)))
    conv = conv_part(padded, kernel, 1)
    group_index = lax.axis_index("seq") % GROUPS
    bias = lax.dynamic_slice_in_dim(conv_bias, group_index * group_width, group_width)
    local = (inputs.astype(jnp.float32) + jax.nn.gelu(conv + bias)).astype(jnp.bfloat16)
    sending = local.reshape(1, per_dev, devices, frame_count, group_width)
    returned = lax.all_to_all(sending, "seq", split_axis=2, concat_axis=0, tiled=True)
    returned = returned.reshape(blocks, GROUPS, per_dev, frame_count, group_width)
    mixed = jnp.transpose(returned, (0, 2, 3, 1, 4)).reshape(rec, frame_count, width)
    heads = w_qkv.shape[2]
    head = w_qkv.shape[3]
    items = rec * heads // devices
    projected = jnp.einsum(
        "btd,dshe->bhtse", mixed, w_qkv, preferred_element_type=jnp.float32
    ).astype(jnp.bfloat16)
    packed = projected.reshape(devices, items, frame_count, 3 * head)
    scale = head ** (-0.5)
    portion = lax.all_to_all(packed, "seq", split_axis=0, concat_axis=2, tiled=True)
    count = portion.shape[1]
    length = portion.shape[2]
    grid = portion.reshape(count, length, 3, head)
    block = math.gcd(length, 512)

    def one(item):
        query = item[:, 0]
        keys = item[:, 1]
        values = item[:, 2]

        def rows(query_block):
            scores = (
                jnp.einsum("qe,ke->qk", query_block, keys, preferred_element_type=jnp.float32)
                * scale
            )
            top = jnp.max(scores, axis=1, keepdims=True)
            weights = jnp.exp(scores - top)
            probs = (weights / jnp.sum(weights, axis=1, keepdims=True)).astype(jnp.bfloat16)
            return jnp.dot(probs, values, preferred_element_type=jnp.float32).astype(jnp.bfloat16)

        return lax.map(rows, query.reshape(length // block, block, head)).reshape(length, head)

    attended = lax.map(one, grid)
    context = lax.all_to_all(attended[None], "seq", split_axis=2, concat_axis=0, tiled=True)
    context = context.reshape(rec, heads, frame_count, head)
    out = jnp.einsum("bhte,hed->btd", context, w_out, preferred_element_type=jnp.float32)
    total = mixed.astype(jnp.float32) + out
    mean = jnp.mean(total, axis=2, keepdims=True)
    centered = total - mean
    var = jnp.mean(centered * centered, axis=2, keepdims=True)
    return (centered / jnp.sqrt(var + 1e-05)).astype(jnp.bfloat16)


def solution(mesh):
    return jax.shard_map(
        body,
        mesh=mesh,
        in_specs=(P("parts", "seq", None), P("seq", None, None), P(), P(), P()),
        out_specs=P("parts", "seq", None),
        check_vma=False,
    )
```

```python
import functools
import math

import jax
import jax.numpy as jnp
from jax import lax
from jax.experimental import pallas as pl
from jax.experimental.pallas import tpu as pltpu
from jax.sharding import PartitionSpec as P

GROUPS = 16
KERNEL = 128
MESH = pl.DeviceIdType.MESH
F32 = jnp.float32
BF16 = jnp.bfloat16


def mm(a, b):
    return jnp.dot(a, b, preferred_element_type=F32)


def pair(a, b):
    w = a.shape[-1] // 2
    return (
        jnp.concatenate([a[:, :w], b[:, :w]], axis=1),
        jnp.concatenate([a[:, w:], b[:, w:]], axis=1),
    )


def fused_kernel(
    n, parts, rec, groups, taps, head,
    x_ref, w_ref, bias_ref, wq_hbm, wo_hbm, out_ref,
    sx, rx, rf, xs, sw, ew, k2, mf, m4, gg, lhs, qacc, qkv, ct, cx, res, rs, wq_ref, wo_ref,
    sx_send, sx_recv, sw_send, sw_recv, f_send, f_recv, z_send, y_send, c_send, g_recv,
    r_send, r_recv, t_send, t_recv, l_sem,
):
    me = lax.axis_index("seq")
    width = x_ref.shape[2]
    frames = x_ref.shape[1]
    gw = width // groups
    pack = 256 // gw
    vs = frames // pack
    rows = rec * vs
    per = n // rec
    wide = width // per
    tap_pairs = w_ref.shape[0] // 2
    share = tap_pairs // parts
    part = lax.axis_index("parts") if parts > 1 else 0
    own_rec = me // per
    own_h = me % per

    barrier = pltpu.get_barrier_semaphore()

    def greet(k, carry):
        pl.semaphore_signal(barrier, inc=1, device_id={"seq": (me + k) % n}, device_id_type=MESH)
        return carry

    lax.fori_loop(1, n, greet, 0)
    for d in range(1, parts):
        pl.semaphore_signal(
            barrier, inc=1, device_id={"parts": (part + d) % parts, "seq": me}, device_id_type=MESH
        )
    wq_load = pltpu.make_async_copy(wq_hbm, wq_ref, l_sem.at[0])
    wo_load = pltpu.make_async_copy(wo_hbm, wo_ref, l_sem.at[1])

    def x_copy(peer, slot):
        return pltpu.make_async_remote_copy(
            src_ref=sx.at[peer], dst_ref=rx.at[slot],
            send_sem=sx_send.at[peer], recv_sem=sx_recv.at[slot],
            device_id={"seq": peer}, device_id_type=MESH,
        )

    def w_copy(peer, slot):
        return pltpu.make_async_remote_copy(
            src_ref=sw.at[peer], dst_ref=ew.at[pl.ds(1 + slot * tap_pairs + part * share, share)],
            send_sem=sw_send.at[peer], recv_sem=sw_recv.at[slot],
            device_id={"seq": peer}, device_id_type=MESH,
        )

    for p in range(share):
        for gp in range(groups // 2):
            tap = 2 * (part * share + p)
            lo, hi = pair(
                w_ref[tap, :, gp * 128:(gp + 1) * 128], w_ref[tap + 1, :, gp * 128:(gp + 1) * 128]
            )
            sw[2 * gp, p] = lo
            sw[2 * gp + 1, p] = hi

    pl.semaphore_wait(barrier, n - 1 + parts - 1)

    def start_w(k, carry):
        w_copy((me + k) % n, me).start()
        return carry

    lax.fori_loop(1, n, start_w, 0)

    ew[pl.ds(1 + me * tap_pairs + part * share, share)] = sw[me]

    def f_copy(d, slot):
        return pltpu.make_async_remote_copy(
            src_ref=ew.at[pl.ds(1 + slot * tap_pairs + part * share, share)],
            dst_ref=ew.at[pl.ds(1 + slot * tap_pairs + part * share, share)],
            send_sem=f_send.at[d - 1, slot], recv_sem=f_recv.at[d - 1, slot],
            device_id={"parts": (part + d) % parts, "seq": me}, device_id_type=MESH,
        )

    def f_wait(d, slot):
        source = (part + parts - d) % parts
        return pltpu.make_async_remote_copy(
            src_ref=ew.at[pl.ds(1 + slot * tap_pairs + source * share, share)],
            dst_ref=ew.at[pl.ds(1 + slot * tap_pairs + source * share, share)],
            send_sem=f_send.at[d - 1, slot], recv_sem=f_recv.at[d - 1, slot],
            device_id={"parts": (part + d) % parts, "seq": me}, device_id_type=MESH,
        )

    for d in range(1, parts):
        f_copy(d, me).start()

    count = rec * frames
    ri = lax.broadcasted_iota(jnp.int32, (count, count), 0)
    ci = lax.broadcasted_iota(jnp.int32, (count, count), 1)
    a_i, rest = ri // rows, ri % rows
    r_i, v_i = rest // vs, rest % vs
    perm = jnp.where(ci == r_i * frames + v_i * pack + a_i, 1.0, 0.0).astype(BF16)
    x2 = x_ref[...].reshape(count, width)
    for gp in range(groups // 2):
        moved = mm(perm, x2[:, gp * 128:(gp + 1) * 128]).astype(BF16)
        for ah in range(pack // 2):
            lo, hi = pair(
                moved[2 * ah * rows:(2 * ah + 1) * rows],
                moved[(2 * ah + 1) * rows:(2 * ah + 2) * rows],
            )
            sx[2 * gp, :, ah * 128:(ah + 1) * 128] = lo
            sx[2 * gp + 1, :, ah * 128:(ah + 1) * 128] = hi

    def start_x(k, carry):
        x_copy((me + k) % n, me).start()
        return carry

    lax.fori_loop(1, n, start_x, 0)
    wq_load.start()
    wo_load.start()
    rx[me] = sx[me]
    ew[0] = jnp.zeros_like(ew[0])
    ew[taps // 2 + 1] = jnp.zeros_like(ew[0])
    zero = jnp.zeros((rows, 128), F32)
    for h in range(2):
        rf[h, 0:rows, :] = zero
        rf[h, (n + 1) * rows:(n + 2) * rows, :] = zero

    def wait_w(k, carry):
        s = (me + n - k) % n
        w_copy(s, s).wait_recv()
        for d in range(1, parts):
            f_copy(d, s).start()
        return carry

    lax.fori_loop(1, n, wait_w, 0)

    def wait_f(k, carry):
        for d in range(1, parts):
            f_wait(d, (me + n - k) % n).wait_recv()
        return carry

    lax.fori_loop(0, n, wait_f, 0)

    blank = jnp.zeros((gw, 128), BF16)
    for j in range(3):
        k2[(taps + 1 + j) * gw:(taps + 2 + j) * gw, 0:128] = blank
    for j in (0, 1, taps + 3):
        k2[j * gw:(j + 1) * gw, 128:256] = blank
    low = lax.broadcasted_iota(jnp.int32, (gw, 128), 1) < gw

    def put(j, val):
        k2[pl.ds(j * gw, gw), 0:128] = val
        k2[pl.ds((j + 2) * gw, gw), 128:256] = val

    def even(p):
        return jnp.where(low, ew[p + 1].astype(F32), ew[p].astype(F32)).astype(BF16)

    def build(p, carry):
        put(2 * p, even(p))
        e = ew[p + 1]
        put(2 * p + 1, jnp.concatenate([e[:, gw:], e[:, :gw]], axis=1))
        return carry

    lax.fori_loop(0, taps // 2, build, 0)
    put(taps, even(taps // 2))

    def widen(k, carry):
        s = (me + n - k) % n

        @pl.when(k > 0)
        def _():
            x_copy(s, s).wait_recv()

        for h in range(2):
            rf[h, pl.ds((s + 1) * rows, rows), :] = rx[s, :, h * 128:(h + 1) * 128].astype(F32)
        return carry

    lax.fori_loop(0, n, widen, 0)

    def spread(k, carry):
        r, v = k // vs, k % vs
        for b in range(3):
            for h in range(2):
                val = rf[h, pl.ds(b * rows + k, n, stride=rows), :].astype(BF16)
                xs[vs * b + v, r, :, h * 128:(h + 1) * 128] = val
        return carry

    lax.fori_loop(0, rows, spread, 0)

    pairs = rec // 2
    chunk = vs * 2 * n
    w2 = bias_ref[:, pl.ds(pl.multiple_of((me // 2) * 128, 128), 128)]
    lo, hi = pair(w2, w2)
    bias = jnp.where(me % 2 == 0, lo, hi)
    bias = jnp.concatenate([bias, bias], axis=1)

    def z_copy(r, slot):
        return pltpu.make_async_remote_copy(
            src_ref=m4.at[r], dst_ref=gg.at[slot],
            send_sem=z_send.at[r], recv_sem=g_recv.at[slot],
            device_id={"seq": r * per + own_h}, device_id_type=MESH,
        )

    for i in range(pairs):
        cp = (own_rec // 2 + 1 + i) % pairs
        acc = jnp.zeros((chunk, 256), F32)
        for q in range(taps // pack + 1):
            acc += mm(
                xs[q:q + vs, pl.ds(2 * cp, 2)].reshape(chunk, 256), k2[q * 256:(q + 1) * 256, :]
            )
        centre = xs[vs:2 * vs, pl.ds(2 * cp, 2)].reshape(chunk, 256).astype(F32)
        mixed = (centre + jax.nn.gelu(acc + bias)).astype(BF16).astype(F32)
        for h in range(2):
            mf[h] = mixed[:, h * 128:(h + 1) * 128]

        def gather(k, carry):
            for h in range(2):
                val = mf[h, pl.ds(k, vs, stride=2 * n), :].astype(BF16)
                m4[2 * cp + k // n, pl.ds((k % n) * vs, vs), h * 128:(h + 1) * 128] = val
            return carry

        lax.fori_loop(0, 2 * n, gather, 0)
        for j in range(2):
            if i < pairs - 1 or j:
                z_copy(2 * cp + (own_rec + j) % 2, me).start()
    gg[me] = m4[own_rec]

    def r_copy(u, slot):
        return pltpu.make_async_remote_copy(
            src_ref=m4.at[:, pl.ds(pl.multiple_of(u * vs, vs), vs)],
            dst_ref=res.at[slot],
            send_sem=r_send.at[u], recv_sem=r_recv.at[slot],
            device_id={"seq": u}, device_id_type=MESH,
        )

    def start_r(k, carry):
        r_copy((me + k) % n, me).start()
        return carry

    lax.fori_loop(1, n, start_r, 0)
    res[me] = m4[:, pl.ds(pl.multiple_of(me * vs, vs), vs), :]
    core, line = own_h % 2, own_h // 2
    lines = per // 2
    sibling = own_rec * per + line * 2 + 1 - core

    def y_copy(d, slot, sem):
        return pltpu.make_async_remote_copy(
            src_ref=gg.at[slot], dst_ref=gg.at[slot],
            send_sem=y_send.at[sem], recv_sem=g_recv.at[slot],
            device_id={"seq": own_rec * per + ((line + d) % lines) * 2 + core}, device_id_type=MESH,
        )

    def c_copy(slot):
        return pltpu.make_async_remote_copy(
            src_ref=gg.at[slot], dst_ref=gg.at[slot],
            send_sem=c_send.at[slot], recv_sem=g_recv.at[slot],
            device_id={"seq": sibling}, device_id_type=MESH,
        )

    wq_load.wait()
    wo_load.wait()
    span = n * vs

    def step_a(e, z):
        slot = z * per + own_h
        if e:
            z_copy(z, slot).wait_recv()
        for d in range(1, lines):
            y_copy(d, slot, (d - 1) * rec + e).start()
        c_copy(slot).start()

    def step_b(e, z):
        for d in range(1, lines):
            slot = z * per + ((line + d) % lines) * 2 + core
            y_copy(d, slot, (d - 1) * rec + e).wait_recv()
            c_copy(slot).start()

    def step_c(e, z):
        for d in range(lines):
            c_copy(z * per + ((line + d) % lines) * 2 + 1 - core).wait_recv()
        for gl in range(per // 2):
            for ah in range(pack // 2):
                g = z * per + 2 * gl
                lo, hi = pair(
                    gg[g, :, ah * 128:(ah + 1) * 128], gg[g + 1, :, ah * 128:(ah + 1) * 128]
                )
                lhs[z, 2 * ah, :, gl * 128:(gl + 1) * 128] = lo
                lhs[z, 2 * ah + 1, :, gl * 128:(gl + 1) * 128] = hi

        def project(a, carry):
            at = pl.ds(a * span, span)
            total = mm(lhs[z, a], wq_ref[pl.ds(pl.multiple_of(z * wide, wide), wide), :])
            if e:
                total += qacc[at, :]
            if e == rec - 1:
                qkv[at, :] = total.astype(BF16)
            else:
                qacc[at, :] = total
            return carry

        lax.fori_loop(0, pack, project, 0)

    mate = (own_rec // 2) * 2 + 1 - own_rec % 2
    others = [
        2 * ((own_rec // 2 + 1 + i) % pairs) + (own_rec + j) % 2
        for i in range(pairs - 1) for j in range(2)
    ]
    zs = list(enumerate([own_rec] + others + [mate]))
    for e, z in zs[:-1]:
        step_a(e, z)
    for e, z in zs[:-1]:
        step_b(e, z)
    step_a(*zs[-1])
    for e, z in zs[:-2]:
        step_c(e, z)
    step_b(*zs[-1])
    for e, z in zs[-2:]:
        step_c(e, z)

    def t_copy(a, u, slot):
        return pltpu.make_async_remote_copy(
            src_ref=ct.at[a, pl.ds(pl.multiple_of(u * vs, vs), vs)],
            dst_ref=cx.at[slot % per, slot // per, a],
            send_sem=t_send.at[a, u], recv_sem=t_recv.at[a, slot],
            device_id={"seq": u}, device_id_type=MESH,
        )

    lane = lax.broadcasted_iota(jnp.int32, (span, wide), 1) // head

    def attend(a, carry):
        query = qkv[pl.ds(a * span, span), 0:wide].astype(F32) * (head ** -0.5)
        done = jnp.zeros((span, wide), F32)
        for h in range(wide // head):
            mine = jnp.where(lane == h, query, 0.0).astype(BF16)
            scores = lax.dot_general(
                mine, qkv[:, wide:2 * wide], (((1,), (1,)), ((), ())), preferred_element_type=F32
            )
            weights = jnp.exp(scores - jnp.max(scores, axis=1, keepdims=True))
            inverse = 1.0 / jnp.sum(weights, axis=1, keepdims=True)
            probs = (weights * inverse).astype(BF16)
            done = jnp.where(lane == h, mm(probs, qkv[:, 2 * wide:3 * wide]), done)
        ct[a] = done.astype(BF16)

        def start_t(k, c):
            t_copy(a, (me + k) % n, me).start()
            return c

        lax.fori_loop(1, n, start_t, 0)
        cx[own_h, own_rec, a] = ct[a, pl.ds(pl.multiple_of(me * vs, vs), vs), :]
        return carry

    lax.fori_loop(0, pack, attend, 0)

    def wait_r(k, carry):
        s = (me + n - k) % n
        r_copy(s, s).wait_recv()
        return carry

    lax.fori_loop(1, n, wait_r, 0)
    for gp in range(groups // 2):
        for ah in range(pack // 2):
            lo, hi = pair(
                res[2 * gp, :, :, ah * 128:(ah + 1) * 128].reshape(rows, 128),
                res[2 * gp + 1, :, :, ah * 128:(ah + 1) * 128].reshape(rows, 128),
            )
            rs[:, 2 * ah, :, gp * 128:(gp + 1) * 128] = lo.reshape(rec, vs, 128)
            rs[:, 2 * ah + 1, :, gp * 128:(gp + 1) * 128] = hi.reshape(rec, vs, 128)

    def wait_t(k, carry):
        s = (me + n - k) % n
        for a in range(pack):
            t_copy(a, s, s).wait_recv()
        return carry

    lax.fori_loop(1, n, wait_t, 0)

    total = mm(cx[0].reshape(count, wide), wo_ref[0:wide, :])
    for b in range(1, per):
        total += mm(cx[b].reshape(count, wide), wo_ref[b * wide:(b + 1) * wide, :])
    total += rs[...].reshape(count, width).astype(F32)
    mean = jnp.mean(total, axis=1, keepdims=True)
    centred = total - mean
    var = jnp.mean(centred * centred, axis=1, keepdims=True)
    normed = (centred / jnp.sqrt(var + 1e-05)).astype(BF16)
    r_o, t_o = ri // frames, ri % frames
    back = jnp.where(ci == r_o * frames + (t_o % pack) * vs + t_o // pack, 1.0, 0.0).astype(BF16)
    out_ref[...] = mm(back, normed).astype(BF16).reshape(rec, frames, width)

    def drain(k, carry):
        s = (me + k) % n
        x_copy(s, me).wait_send()
        w_copy(s, me).wait_send()
        r_copy(s, me).wait_send()
        for a in range(pack):
            t_copy(a, s, me).wait_send()
        return carry

    lax.fori_loop(1, n, drain, 0)
    for d in range(1, parts):
        for s in range(n):
            f_copy(d, s).wait_send()
    for e, z in zs:
        if e:
            z_copy(z, me).wait_send()
        for d in range(1, lines):
            y_copy(d, z * per + own_h, (d - 1) * rec + e).wait_send()
        for d in range(lines):
            c_copy(z * per + ((line + d) % lines) * 2 + core).wait_send()


def fused(n, frames, conv_weight, conv_bias, w_qkv, w_out):
    rec, frame_count, width = frames.shape
    heads, head = w_qkv.shape[2:]
    groups, taps = GROUPS, KERNEL
    gw = width // groups
    pack = 256 // gw
    vs = frame_count // pack
    rows = rec * vs
    per = n // rec
    wide = width // per
    tap_pairs = conv_weight.shape[0] // 2
    me = lax.axis_index("seq")
    mine = heads // per
    w_mine = lax.dynamic_slice_in_dim(w_qkv, (me % per) * mine, mine, 2).reshape(width, 3 * mine * head)
    bias = conv_bias.reshape(1, width)
    parts = lax.axis_size("parts")
    if tap_pairs % parts:
        parts = 1
    vm = lambda *s: pltpu.VMEM(s, BF16)
    dma = lambda *s: pltpu.SemaphoreType.DMA(s)
    lines = per // 2
    return pl.pallas_call(
        functools.partial(fused_kernel, n, parts, rec, groups, taps, head),
        out_shape=jax.ShapeDtypeStruct(frames.shape, BF16),
        in_specs=[pl.BlockSpec(memory_space=pltpu.VMEM)] * 3 + [pl.BlockSpec(memory_space=pl.ANY)] * 2,
        out_specs=pl.BlockSpec(memory_space=pltpu.VMEM),
        scratch_shapes=[
            vm(n, rows, 256), vm(n, rows, 256), pltpu.VMEM((2, (n + 2) * rows, 128), F32),
            vm(3 * vs, rec, n, 256), vm(n, tap_pairs // parts, gw, 128), vm(taps // 2 + 2, gw, 128),
            vm((taps + 4) * gw, 256), pltpu.VMEM((2, vs * 2 * n, 128), F32),
            vm(rec, n * vs, 256), vm(n, n * vs, 256), vm(per, pack, n * vs, wide),
            pltpu.VMEM((pack * n * vs, 3 * wide), F32), vm(pack * n * vs, 3 * wide), vm(pack, n * vs, wide),
            vm(per, rec, pack, vs, wide), vm(n, rec, vs, 256), vm(rec, pack, vs, width),
            vm(width, 3 * wide), vm(width, width),
            dma(n), dma(n), dma(n), dma(n),
            dma(max(1, parts - 1), n), dma(max(1, parts - 1), n), dma(rec), dma(max(1, (lines - 1) * rec)), dma(n), dma(n),
            dma(n), dma(n), dma(pack, n), dma(pack, n), dma(2),
        ],
        compiler_params=pltpu.CompilerParams(
            collective_id=0, has_side_effects=True, vmem_limit_bytes=56 * 2 ** 20
        ),
    )(frames, conv_weight, bias, w_mine, w_out.reshape(width, width))


def conv_part(source, kernel, groups):
    return lax.conv_general_dilated(
        source,
        kernel,
        (1,),
        "VALID",
        dimension_numbers=("NWC", "WIO", "NWC"),
        feature_group_count=groups,
        preferred_element_type=jnp.float32,
    )


def fits(n, frames, conv_weight, w_qkv):
    rec, frame_count, width = frames.shape
    heads, head = w_qkv.shape[2:]
    return (
        n == GROUPS
        and width == heads * head
        and width == GROUPS * 64
        and frame_count == KERNEL // 2
        and n % (2 * rec) == 0
        and rec % 2 == 0
        and n * 64 == 256 * rec
        and conv_weight.shape[0] % 2 == 0
        and heads % (n // rec) == 0
        and width * rec == 256 * n
    )


def body(frames, conv_weight, conv_bias, w_qkv, w_out):
    rec, frame_count, width = frames.shape
    devices = lax.axis_size("seq")
    if fits(devices, frames, conv_weight, w_qkv):
        return fused(devices, frames, conv_weight, conv_bias, w_qkv, w_out)
    group_width = width // GROUPS
    half = KERNEL // 2
    blocks = devices // GROUPS
    per_dev = rec // blocks
    tap_count = conv_weight.shape[0]
    spread = conv_weight.reshape(tap_count, group_width, 1, GROUPS, group_width)
    spread = jnp.broadcast_to(spread, (tap_count, group_width, blocks, GROUPS, group_width))
    spread = spread.reshape(tap_count, group_width, devices, group_width)
    kernel = lax.all_to_all(spread, "seq", split_axis=2, concat_axis=0, tiled=True).reshape(
        KERNEL, group_width, group_width
    )
    arranged = frames.reshape(blocks, per_dev, frame_count, GROUPS, group_width)
    arranged = jnp.transpose(arranged, (0, 3, 1, 2, 4)).reshape(
        devices, per_dev, frame_count, group_width
    )
    length = frame_count * devices
    inputs = lax.all_to_all(arranged, "seq", split_axis=0, concat_axis=2, tiled=True).reshape(
        per_dev, length, group_width
    )
    padded = jnp.pad(inputs, ((0, 0), (half, half - 1), (0, 0)))
    conv = conv_part(padded, kernel, 1)
    group_index = lax.axis_index("seq") % GROUPS
    bias = lax.dynamic_slice_in_dim(conv_bias, group_index * group_width, group_width)
    local = (inputs.astype(jnp.float32) + jax.nn.gelu(conv + bias)).astype(jnp.bfloat16)
    sending = local.reshape(1, per_dev, devices, frame_count, group_width)
    returned = lax.all_to_all(sending, "seq", split_axis=2, concat_axis=0, tiled=True)
    returned = returned.reshape(blocks, GROUPS, per_dev, frame_count, group_width)
    mixed = jnp.transpose(returned, (0, 2, 3, 1, 4)).reshape(rec, frame_count, width)
    heads = w_qkv.shape[2]
    head = w_qkv.shape[3]
    items = rec * heads // devices
    projected = jnp.einsum(
        "btd,dshe->bhtse", mixed, w_qkv, preferred_element_type=jnp.float32
    ).astype(jnp.bfloat16)
    packed = projected.reshape(devices, items, frame_count, 3 * head)
    scale = head ** (-0.5)
    portion = lax.all_to_all(packed, "seq", split_axis=0, concat_axis=2, tiled=True)
    count = portion.shape[1]
    length = portion.shape[2]
    grid = portion.reshape(count, length, 3, head)
    block = math.gcd(length, 512)

    def one(item):
        query = item[:, 0]
        keys = item[:, 1]
        values = item[:, 2]

        def rows(query_block):
            scores = (
                jnp.einsum("qe,ke->qk", query_block, keys, preferred_element_type=jnp.float32)
                * scale
            )
            top = jnp.max(scores, axis=1, keepdims=True)
            weights = jnp.exp(scores - top)
            probs = (weights / jnp.sum(weights, axis=1, keepdims=True)).astype(jnp.bfloat16)
            return jnp.dot(probs, values, preferred_element_type=jnp.float32).astype(jnp.bfloat16)

        return lax.map(rows, query.reshape(length // block, block, head)).reshape(length, head)

    attended = lax.map(one, grid)
    context = lax.all_to_all(attended[None], "seq", split_axis=2, concat_axis=0, tiled=True)
    context = context.reshape(rec, heads, frame_count, head)
    out = jnp.einsum("bhte,hed->btd", context, w_out, preferred_element_type=jnp.float32)
    total = mixed.astype(jnp.float32) + out
    mean = jnp.mean(total, axis=2, keepdims=True)
    centered = total - mean
    var = jnp.mean(centered * centered, axis=2, keepdims=True)
    return (centered / jnp.sqrt(var + 1e-05)).astype(jnp.bfloat16)


def solution(mesh):
    return jax.shard_map(
        body,
        mesh=mesh,
        in_specs=(P("parts", "seq", None), P("seq", None, None), P(), P(), P()),
        out_specs=P("parts", "seq", None),
        check_vma=False,
    )
```
